32 devices in a mesh: parts: 2 (over x), seq: 16 (over z, y, core).
Axes of the slice: x: 2, y: 2, z: 4, core: 2. Of those that a mesh axis runs over, the one named last changes fastest.
Arguments:
- queries: bfloat16 [4096, 1024], P(('parts', 'seq')), parts along dimension 0, may hold values from -6 to 6
- keys: bfloat16 [4096, 1024], P(('parts', 'seq')), parts along dimension 0, may hold values from -6 to 6
- values: bfloat16 [4096, 1024], P(('parts', 'seq')), parts along dimension 0, may hold values from -6 to 6
- log_forget: float32 [8, 4096], P(None, ('parts', 'seq')), parts along dimension 1, may hold values from -5 to 0
- input_gate: float32 [8, 4096], P(None, ('parts', 'seq')), parts along dimension 1, may hold values from 0.1 to 1
- ridge: float32 [8], replicated, may hold values from 0.25 to 4
- gain: float32 [1024], replicated, may hold values from 0.25 to 1.75
- out_weight: bfloat16 [1024, 2048], P('seq'), may hold values from -0.1875 to 0.1875
Outputs:
- mixed: bfloat16 [4096, 2048], P(('parts', 'seq')), parts along dimension 0
The draws below stay inside these ranges and needn't reach their ends.
There are 2 independent parts, one for each index of `parts`. The reference program is written for one: setup_inputs(seed, part) draws one part's arguments, and reference() takes and returns one part's arrays. A program takes and returns all parts, laid end to end along the dimension named above; an argument that names none is the same for every part. Nothing has to cross between parts.
All inputs are finite; a program needn't handle non-finite values. Where the reference program divides by a largest or mean magnitude, that divisor is 1e-20 or more.
Results may differ from the reference program's by a relative error of at most 0.007.
Values may be sent and summed in bfloat16 or wider, within the bound.
A program may use at most 192 MiB of HBM per device.

```python
import math
import jax
import jax.numpy as jnp
from jax import lax

D = 2048
HEADS = 8
DH = 128
C = 128
NEWTON = 6
CORR = 4
TOK_DEV = 128
SEQ = 2048
HD = 1024


def draw_log_forget(key, part):
    streams = jax.random.split(jax.random.fold_in(key, 71), 6)
    order = jax.random.permutation(streams[0], HEADS)
    half = HEADS // 2
    sections = SEQ // TOK_DEV
    slow_rate = jnp.exp(jax.random.uniform(streams[1], (HEADS,), jnp.float32, math.log(0.1), math.log(0.6))) / SEQ
    spread_count = max(HEADS - half - 1, 1)
    rank = jnp.maximum(order - half, 0).astype(jnp.float32) / spread_count
    quick_rate = jnp.exp(math.log(14.0) + rank * (math.log(0.5) - math.log(14.0))) / TOK_DEV
    is_slow = order < half
    rate = jnp.where(is_slow, slow_rate, quick_rate)
    section_scale = jnp.exp(jax.random.uniform(streams[2], (HEADS, sections, 1), jnp.float32, math.log(0.5), math.log(2.0)))
    token_scale = jnp.exp(jax.random.uniform(streams[3], (HEADS, sections, TOK_DEV), jnp.float32, math.log(0.5), math.log(2.0)))
    starting_offset = -(rate[:, None, None] * section_scale * token_scale).reshape(HEADS, SEQ)
    sample_locations = jax.random.randint(streams[4], (HEADS, 2), 0, SEQ)
    loss_values = jnp.log(jax.random.uniform(streams[5], (HEADS, 2), jnp.float32, 0.5, 0.8))
    token_positions = jnp.arange(SEQ)[None, :]
    token_group = jnp.where(token_positions == sample_locations[:, 0:1], loss_values[:, 0:1], 0.0) + jnp.where(token_positions == sample_locations[:, 1:2], loss_values[:, 1:2], 0.0)
    return starting_offset + token_group


def levels(key, shape, cuts, low, top_value):
    def one(dim, shards_of):
        heights = jax.random.uniform(jax.random.fold_in(jax.random.fold_in(key, 6), dim), (shards_of,), jnp.float32, low / len(cuts), top_value / len(cuts))
        return jnp.repeat(jnp.exp(heights), shape[dim] // shards_of).reshape((-1,) + (1,) * (len(shape) - dim - 1))

    level = one(*cuts[0])
    for cut in cuts[1:]:
        level = level * one(*cut)
    return level


def scatter_about(stream_key, dims, scale, limit, shards=(), kind=jnp.bfloat16):
    drawn = jax.random.normal(stream_key, dims, jnp.float32) * scale
    if len(shards) > 0:
        drawn = levels(stream_key, dims, shards, -0.22, 0.18) * drawn
    return jnp.clip(drawn, min=-limit, max=limit).astype(kind)


def setup_inputs(seed: int = 0, part: int = 0) -> dict:
    streams_of = jax.random.split(jax.random.key(seed), 9)
    part_keys = jax.random.split(jax.random.fold_in(streams_of[8], part), 9)
    queries = scatter_about(part_keys[0], (SEQ, HD), 1.0, 6.0, ((0, 16),))
    keys = scatter_about(part_keys[1], (SEQ, HD), 1.0, 6.0, ((0, 16),))
    values = scatter_about(part_keys[2], (SEQ, HD), 1.0, 6.0, ((0, 16),))
    log_forget = draw_log_forget(jax.random.fold_in(jax.random.fold_in(streams_of[8], part), 71), part)
    input_gate = jnp.clip(0.1 + 0.9 * jax.random.uniform(part_keys[4], (HEADS, SEQ), jnp.float32) ** levels(part_keys[4], (HEADS, SEQ), ((1, 16),), -0.2, 0.2), 0.1, 1.0)
    ridge = jnp.clip(jnp.exp(jax.random.uniform(streams_of[5], (HEADS,), jnp.float32, math.log(0.25), math.log(4.0))), 0.25, 4.0)
    gain = jnp.clip(1.0 + 0.15 * jax.random.normal(streams_of[6], (HD,), jnp.float32), 0.25, 1.75)
    out_weight = scatter_about(streams_of[7], (HD, D), HD ** -0.5, 0.1875, ((0, 16),))
    return dict(queries=queries, keys=keys, values=values, log_forget=log_forget, input_gate=input_gate, ridge=ridge, gain=gain, out_weight=out_weight)


highest = lax.Precision.HIGHEST

def product(left, right):
    return jnp.matmul(left, right, precision=highest)

def unit_rows(field):
    return field * lax.rsqrt(lax.optimization_barrier(jnp.sum(field * field, axis=-1, keepdims=True)) + 1e-06)

def newton_inverse(system):
    bound = lax.optimization_barrier(jnp.max(lax.optimization_barrier(jnp.sum(jnp.abs(system), axis=-1)), axis=-1))
    identity = jnp.eye(system.shape[-1], dtype=system.dtype)
    approx = identity / bound[..., None, None]
    for iteration in range(NEWTON):
        approx = product(approx, 2.0 * identity - product(system, approx))
    return approx

def solve_block(query_rows, key_rows, beta_keys, start_gram, pre_gram, decay_row, mixing, ridge_col):
    identity = jnp.eye(query_rows.shape[-1], dtype=query_rows.dtype)
    system = start_gram + pre_gram + ridge_col * identity
    inverse = newton_inverse(system)
    solved = product(query_rows, inverse)
    key_t = jnp.swapaxes(key_rows, -1, -2)
    for iteration in range(CORR - 1):
        attention_scores = mixing * product(solved, key_t)
        applied = decay_row * product(solved, start_gram) + product(attention_scores, beta_keys) + ridge_col * solved
        solved = solved + product(query_rows - applied, inverse)
    attention_scores = mixing * product(solved, key_t)
    return (solved, attention_scores)

def reference(queries, keys, values, log_forget, input_gate, ridge, gain, out_weight):
    total = queries.shape[0]
    count = total // C

    def blocks(field):
        return field.astype(jnp.float32).reshape(count, C, HEADS, DH).transpose(0, 2, 1, 3)

    def gate_blocks(field):
        return field.reshape(HEADS, count, C).transpose(1, 0, 2)
    query_all = unit_rows(blocks(queries))
    key_all = unit_rows(blocks(keys))
    value_all = blocks(values)
    forget_all = gate_blocks(log_forget)
    beta_all = gate_blocks(input_gate)
    lower_mask = jnp.tril(jnp.ones((C, C), query_all.dtype))
    ridge_col = ridge[:, None, None]

    def advance(carry, items):
        gram_sum, state_sum = carry
        query_rows, key_rows, value_rows, forget_rows, gate_rows = items
        running = jnp.cumsum(forget_rows, axis=-1)
        last = running[:, -1:]
        decay_row = jnp.exp(running)[..., None]
        mixing = lower_mask * jnp.exp(jnp.minimum(running[:, :, None] - running[:, None, :], 0.0))
        tail = (jnp.exp(last - running) * gate_rows)[..., None]
        beta_keys = gate_rows[..., None] * key_rows
        beta_values = gate_rows[..., None] * value_rows
        key_t = jnp.swapaxes(key_rows, -1, -2)
        block_gram = product(key_t, tail * key_rows)
        state_per_block = product(key_t, tail * value_rows)
        pre_gram = product(key_t, beta_keys)
        solved, attention_scores = solve_block(query_rows, key_rows, beta_keys, gram_sum, pre_gram, decay_row, mixing, ridge_col)
        output = decay_row * product(solved, state_sum) + product(attention_scores, beta_values)
        shrink = jnp.exp(last)[..., None]
        return ((shrink * gram_sum + block_gram, shrink * state_sum + state_per_block), output)
    start = (jnp.zeros((HEADS, DH, DH), query_all.dtype), jnp.zeros((HEADS, DH, DH), query_all.dtype))
    carry, outputs = lax.scan(advance, start, (query_all, key_all, value_all, forget_all, beta_all))
    normed = outputs * lax.rsqrt(lax.optimization_barrier(jnp.mean(outputs * outputs, axis=-1, keepdims=True)) + 1e-06)
    normed = normed.transpose(0, 2, 1, 3).reshape(total, HEADS * DH) * gain
    normed = normed.astype(jnp.bfloat16)
    return jnp.dot(normed, out_weight, preferred_element_type=jnp.float32).astype(jnp.bfloat16)
```

```python
import functools

import jax
import jax.numpy as jnp
from jax import lax
from jax.experimental import pallas as pl
from jax.experimental.pallas import tpu as pltpu
from jax.sharding import PartitionSpec as P

NEWTON = 6
CORR = 4
EPS = 1e-06
F32 = jnp.float32
BF16 = jnp.bfloat16
MESH = pl.DeviceIdType.MESH
HIGHEST = lax.Precision.HIGHEST


def dot(a, b, dims=((1,), (0,)), precision=None):
    return lax.dot_general(a, b, (dims, ((), ())), precision=precision, preferred_element_type=F32)


def low(a):
    return a.astype(BF16)


def split_dot(a, b):
    high = low(a)
    return dot(high, b) + dot(low(a - high.astype(F32)), b)


def kernel(
    layers, ring, heads, q_ref, k_ref, v_ref, forget_ref, gate_ref, ridge_ref, gain_ref, w_ref,
    out_ref, level, gram_out, gram_in, gram_chain_in, gram_chain_out, gram_back, gram_full,
    state_out, state_in, state_chain_in, state_chain_out, state_back, state_full,
    weights, y_ref,
    level_sems, piece_sems, chain_sems, back_sems, z_sems, y_sems, core_sems,
):
    me = lax.axis_index("seq")
    layer, rank = me // ring, me % ring
    share = heads // ring
    tokens = q_ref.shape[0]
    dh = q_ref.shape[1] // heads
    rows = w_ref.shape[0]
    pending = []

    def others():
        return [(rank + d) % ring for d in range(1, ring)]

    def send(src, dst, sems, slot_out, slot_in, target):
        copy = pltpu.make_async_remote_copy(
            src_ref=src, dst_ref=dst, send_sem=sems[0].at[slot_out], recv_sem=sems[1].at[slot_in],
            device_id={"seq": target}, device_id_type=MESH,
        )
        copy.start()
        return copy

    def arrived(dst, sems, slot):
        pltpu.make_async_remote_copy(
            src_ref=dst, dst_ref=dst, send_sem=sems[0].at[slot], recv_sem=sems[1].at[slot],
            device_id={"seq": (me + 1) % (layers * ring)}, device_id_type=MESH,
        ).wait_recv()

    def shard(index):
        return weights.at[pl.ds(pl.multiple_of(index * rows, rows), rows)]

    barrier = pltpu.get_barrier_semaphore()
    partners = [layer * ring + p for p in others()]
    partners += [((layer + d) % layers) * ring + rank for d in range(1, layers)]
    for partner in partners:
        pl.semaphore_signal(barrier, inc=1, device_id={"seq": partner}, device_id_type=MESH)
    pl.semaphore_wait(barrier, len(partners))

    row_id = lax.broadcasted_iota(jnp.int32, (tokens, tokens), 0)
    col_id = lax.broadcasted_iota(jnp.int32, (tokens, tokens), 1)
    upper = (row_id <= col_id).astype(F32)
    lower = row_id >= col_id
    eye = (row_id == col_id).astype(F32)
    forget = forget_ref[...]
    run_row = dot(forget, upper, precision=HIGHEST)
    run_col = dot(lower.astype(F32), forget, ((1,), (1,)), precision=HIGHEST)
    gate_col = dot(eye, gate_ref[...], ((1,), (1,)), precision=HIGHEST)
    last = jnp.sum(forget, axis=1, keepdims=True)
    level[rank] = jnp.broadcast_to(last, (heads, dh))
    for p in others():
        pending.append(send(level.at[rank], level.at[rank], level_sems, p, rank, layer * ring + p))

    across = (rank + ring // 2) % ring
    sibling = rank + 1 - 2 * (rank % 2)
    pending.append(send(w_ref, shard(me), y_sems, layer, layer, layer * ring + across))
    pending.append(send(w_ref, shard(me), core_sems, layer * 2, layer * 2 + rank // 2, layer * ring + sibling))

    def to_column():
        for d in range(1, layers):
            there = (layer + d) % layers
            pending.append(send(w_ref, shard(me), z_sems, there, layer, there * ring + rank))

    def from_column(d):
        there = (layer + d) % layers
        piece = shard(there * ring + rank)
        arrived(piece, z_sems, there)
        pending.append(send(piece, piece, y_sems, there, there, layer * ring + across))
        pending.append(send(piece, piece, core_sems, there * 2, there * 2 + rank // 2, layer * ring + sibling))

    def from_across(d):
        there = (layer + d) % layers
        piece = shard(there * ring + across)
        arrived(piece, y_sems, there)
        pending.append(send(piece, piece, core_sems, there * 2 + 1, there * 2 + across // 2, layer * ring + sibling))

    pre, keys_t, keys_low, beta_keys = [], [], [], []
    mixes, decays = [], []
    for h in range(heads):
        lanes = slice(h * dh, (h + 1) * dh)
        raw = k_ref[:, lanes]
        key = raw.astype(F32)
        scale = lax.rsqrt(jnp.sum(key * key, axis=1, keepdims=True) + EPS)
        beta = gate_col[:, h:h + 1]
        run = run_col[:, h:h + 1]
        tail = jnp.exp(last[h:h + 1, :] - run) * beta
        value = v_ref[:, lanes].astype(F32)
        unit = scale * key
        right = jnp.concatenate(
            [low((tail * scale) * unit), low((beta * scale) * unit), low((tail * scale) * value),
             low(scale * eye)], axis=1)
        made = dot(raw, right, ((0,), (0,)))
        gram_out[h] = low(made[:, :dh])
        pre.append(made[:, dh:2 * dh])
        state_out[h] = made[:, 2 * dh:3 * dh]
        keys_t.append(low(made[:, 3 * dh:]))
        beta_keys.append(low(beta * unit))
        mixes.append(jnp.where(lower, jnp.exp(jnp.minimum(run - run_row[h:h + 1, :], 0.0)), 0.0))
        decays.append(jnp.exp(run))

    mine = pl.ds(rank * share, share)
    kinds = (
        (gram_out, gram_in, gram_chain_in, gram_chain_out, gram_back, gram_full, 0),
        (state_out, state_in, state_chain_in, state_chain_out, state_back, state_full, 1),
    )

    def sems_of(sems, kind):
        return (sems[0].at[kind], sems[1].at[kind])

    for outgoing, incoming, *_, kind in kinds:
        for p in others():
            pending.append(send(
                outgoing.at[pl.ds(p * share, share)], incoming.at[rank],
                sems_of(piece_sems, kind), p, rank, layer * ring + p))
        incoming[rank] = outgoing[mine]
    to_column()

    for p in others():
        arrived(level.at[p], level_sems, p)
    chained = []

    def scan(outgoing, incoming, chain_in, chain_out, back, full, kind):
        for p in others():
            arrived(incoming.at[p], sems_of(piece_sems, kind), p)
        kept = incoming.dtype
        shrink, total = [], []
        for j in range(share):
            steps = [jnp.exp(level[p, pl.ds(rank * share + j, 1), :]) for p in range(ring)]
            whole = jnp.zeros((dh, dh), F32)
            for p in range(ring):
                whole = steps[p] * whole + incoming[p, j].astype(F32)
            shrink.append(steps)
            total.append(whole)

        @pl.when(layer == 0)
        def _():
            chain_in[...] = jnp.zeros_like(chain_in)

        for j in range(share):
            @pl.when(layer > 0)
            def _():
                arrived(chain_in.at[j], sems_of(chain_sems, kind), j)

            @pl.when(layer < layers - 1)
            def _():
                steps = shrink[j]
                over = steps[0]
                for p in range(1, ring):
                    over = over * steps[p]
                chain_out[j] = (over * chain_in[j].astype(F32) + total[j]).astype(kept)
                send(chain_out.at[j], chain_in.at[j], sems_of(chain_sems, kind), j, j, me + ring)
        for j in range(share):
            current = chain_in[j].astype(F32)
            for p in range(ring):
                back[p, j] = current.astype(kept)
                if p < ring - 1:
                    current = shrink[j][p] * current + incoming[p, j].astype(F32)
        for p in others():
            pending.append(send(back.at[p], full.at[mine], sems_of(back_sems, kind), p, rank, layer * ring + p))
        full[mine] = back[rank]
        chained.append((chain_out, chain_in, kind))

    scan(*kinds[0])
    scan(*kinds[1])
    for p in others():
        arrived(gram_full.at[pl.ds(p * share, share)], sems_of(back_sems, 0), p)
    ahead = list(range(1, layers))
    if ahead:
        from_column(ahead.pop(0))

    starts = [gram_full[h] for h in range(heads)]
    systems, inverses, bounds = [], [], []
    for h in range(heads):
        system = starts[h].astype(F32) + pre[h] + ridge_ref[h] * eye
        bound = jnp.max(jnp.sum(jnp.abs(system), axis=0, keepdims=True), axis=1, keepdims=True)
        inv = 1.0 / bound
        inverses.append(low((2.0 * eye - system * inv) * inv))
        systems.append(low(system))
    for step in range(NEWTON - 1):
        rests = [low(2.0 * eye - dot(systems[h], inverses[h])) for h in range(heads)]
        inverses = [low(dot(inverses[h], rests[h])) for h in range(heads)]
    from_across(0)
    if ahead:
        from_column(ahead.pop(0))

    both = [jnp.concatenate([starts[h], keys_t[h]], axis=1) for h in range(heads)]
    queries, solved = [], []
    for h in range(heads):
        query = q_ref[:, h * dh:(h + 1) * dh].astype(F32)
        query = query * lax.rsqrt(jnp.sum(query * query, axis=1, keepdims=True) + EPS)
        queries.append(query)
        solved.append(dot(low(query), inverses[h]))
    done = 1
    for step in range(CORR - 1):
        for h in range(heads):
            joint = dot(low(solved[h]), both[h])
            applied = (
                decays[h] * joint[:, :dh]
                + dot(low(mixes[h] * joint[:, dh:]), beta_keys[h])
                + ridge_ref[h] * solved[h]
            )
            solved[h] = solved[h] + dot(low(queries[h] - applied), inverses[h])
        while ahead and (step == CORR - 2 or len(ahead) > CORR - 2 - step):
            from_column(ahead.pop(0))
        if done < layers:
            from_across(done)
            done += 1
    while done < layers:
        from_across(done)
        done += 1

    for p in others():
        arrived(state_full.at[pl.ds(p * share, share)], sems_of(back_sems, 1), p)
    for h in range(heads):
        lanes = slice(h * dh, (h + 1) * dh)
        scores = mixes[h] * split_dot(solved[h], keys_t[h])
        value = low(gate_col[:, h:h + 1] * v_ref[:, lanes].astype(F32))
        state = state_full[h]
        output = decays[h] * split_dot(solved[h], low(state)) + dot(low(scores), value)
        output = output + decays[h] * dot(low(solved[h]), low(state - low(state).astype(F32)))
        norm = lax.rsqrt(jnp.mean(output * output, axis=1, keepdims=True) + EPS)
        y_ref[:, lanes] = low(output * norm * gain_ref[:, lanes])

    weights[pl.ds(pl.multiple_of(me * rows, rows), rows), :] = w_ref[...]
    other = sibling
    for there in range(layers):
        for half in range(ring // 2):
            arrived(shard(there * ring + half * 2 + other % 2), core_sems, there * 2 + half)
    columns = w_ref.shape[1]
    width = min(512, columns)
    for c in range(0, columns, width):
        out_ref[:, c:c + width] = low(dot(y_ref[...], weights[:, c:c + width]))

    for copy in pending:
        copy.wait_send()
    for chain_out, chain_in, kind in chained:
        @pl.when(layer < layers - 1)
        def _():
            for j in range(share):
                sems = sems_of(chain_sems, kind)
                pltpu.make_async_remote_copy(
                    src_ref=chain_out.at[j], dst_ref=chain_in.at[j], send_sem=sems[0].at[j],
                    recv_sem=sems[1].at[j], device_id={"seq": me + ring}, device_id_type=MESH,
                ).wait_send()


def wrapped(body, *refs):
    tail = refs[-14:]
    pairs = [(tail[i], tail[i + 1]) for i in range(0, 14, 2)]
    body(*refs[:-14], *pairs)


def solution(mesh):
    n = mesh.shape["seq"]
    ring = 4
    layers = n // ring

    def on_device(queries, keys, values, log_forget, input_gate, ridge, gain, out_weight):
        tokens, features = queries.shape
        heads = log_forget.shape[0]
        dh = features // heads
        share = heads // ring
        rows, columns = out_weight.shape

        def scans(kind):
            return [
                pltpu.VMEM((heads, dh, dh), kind),
                pltpu.VMEM((ring, share, dh, dh), kind),
                pltpu.VMEM((share, dh, dh), kind),
                pltpu.VMEM((share, dh, dh), kind),
                pltpu.VMEM((ring, share, dh, dh), kind),
                pltpu.VMEM((heads, dh, dh), kind),
            ]

        def pair(*shape):
            return [pltpu.SemaphoreType.DMA(shape), pltpu.SemaphoreType.DMA(shape)]

        vmem = pl.BlockSpec(memory_space=pltpu.VMEM)
        smem = pl.BlockSpec(memory_space=pltpu.SMEM)
        return pl.pallas_call(
            functools.partial(wrapped, functools.partial(kernel, layers, ring, heads)),
            out_shape=jax.ShapeDtypeStruct((tokens, columns), BF16),
            in_specs=[vmem, vmem, vmem, vmem, vmem, smem, vmem, vmem],
            out_specs=vmem,
            scratch_shapes=[
                pltpu.VMEM((ring, heads, dh), F32),
                *scans(BF16),
                *scans(F32),
                pltpu.VMEM((n * rows, columns), BF16),
                pltpu.VMEM((tokens, features), BF16),
                *pair(ring),
                *pair(2, ring),
                *pair(2, share),
                *pair(2, ring),
                *pair(layers),
                *pair(layers),
                *pair(layers * 2),
            ],
            compiler_params=pltpu.CompilerParams(
                collective_id=0, has_side_effects=True, vmem_limit_bytes=48 * 1024 * 1024),
        )(queries, keys, values, log_forget, input_gate, ridge, gain.reshape(1, features), out_weight)

    placed = (
        P(("parts", "seq"), None),
        P(("parts", "seq"), None),
        P(("parts", "seq"), None),
        P(None, ("parts", "seq")),
        P(None, ("parts", "seq")),
        P(),
        P(),
        P("seq", None),
    )
    return jax.shard_map(
        on_device, mesh=mesh, in_specs=placed, out_specs=P(("parts", "seq"), None), check_vma=False
    )
```

```python
import functools

import jax
import jax.numpy as jnp
from jax import lax
from jax.experimental import pallas as pl
from jax.experimental.pallas import tpu as pltpu
from jax.sharding import PartitionSpec as P

NEWTON = 6
CORR = 4
EPS = 1e-06
F32 = jnp.float32
BF16 = jnp.bfloat16
MESH = pl.DeviceIdType.MESH
HIGHEST = lax.Precision.HIGHEST


def dot(a, b, dims=((1,), (0,)), precision=None):
    return lax.dot_general(a, b, (dims, ((), ())), precision=precision, preferred_element_type=F32)


def low(a):
    return a.astype(BF16)


def split_dot(a, b):
    high = low(a)
    return dot(high, b) + dot(low(a - high.astype(F32)), b)


def kernel(
    layers, ring, heads, q_hbm, k_hbm, v_hbm, forget_hbm, gate_hbm, ridge_ref, gain_hbm, w_ref,
    out_ref, q_ref, k_ref, v_ref, forget_ref, gate_ref, gain_ref, load_sems, level, gram_out, gram_in, gram_chain_in, gram_chain_out, gram_back, gram_full,
    state_out, state_in, state_chain_in, state_chain_out, state_back, state_full,
    weights, y_ref,
    level_sems, piece_sems, chain_sems, back_sems, z_sems, y_sems, x_sems, core_sems,
):
    me = lax.axis_index("seq")
    layer, rank = me // ring, me % ring
    share = heads // ring
    tokens = q_ref.shape[0]
    dh = q_ref.shape[1] // heads
    rows, columns = w_ref.shape
    half = columns // 2
    part = lax.axis_index("parts")
    side = part % 2
    twin = part + 1 - 2 * side
    pending = []

    def others():
        return [(rank + d) % ring for d in range(1, ring)]

    def send(src, dst, sems, slot_out, slot_in, target, where=None):
        copy = pltpu.make_async_remote_copy(
            src_ref=src, dst_ref=dst, send_sem=sems[0].at[slot_out], recv_sem=sems[1].at[slot_in],
            device_id={"seq": target} if where is None else {"parts": where, "seq": target},
            device_id_type=MESH,
        )
        copy.start()
        return copy

    def arrived(dst, sems, slot):
        pltpu.make_async_remote_copy(
            src_ref=dst, dst_ref=dst, send_sem=sems[0].at[slot], recv_sem=sems[1].at[slot],
            device_id={"seq": (me + 1) % (layers * ring)}, device_id_type=MESH,
        ).wait_recv()

    def piece_of(ref, index, part_side):
        return ref.at[pl.ds(pl.multiple_of(index * rows, rows), rows),
                      pl.ds(pl.multiple_of(part_side * half, 128), half)]

    loads = []
    for i, (src, dst) in enumerate((
        (forget_hbm, forget_ref), (gate_hbm, gate_ref), (k_hbm, k_ref), (v_hbm, v_ref), (q_hbm, q_ref),
        (gain_hbm, gain_ref), (w_ref, weights.at[pl.ds(pl.multiple_of(me * rows, rows), rows)]),
    )):
        loads.append(pltpu.make_async_copy(src, dst, load_sems.at[i]))
        loads[-1].start()

    barrier = pltpu.get_barrier_semaphore()
    partners = [layer * ring + p for p in others()]
    partners += [((layer + d) % layers) * ring + rank for d in range(1, layers)]
    for partner in partners:
        pl.semaphore_signal(barrier, inc=1, device_id={"seq": partner}, device_id_type=MESH)
    pl.semaphore_signal(
        barrier, inc=1, device_id={"parts": twin, "seq": me}, device_id_type=MESH)
    pl.semaphore_wait(barrier, len(partners) + 1)
    for load in loads[:4]:
        load.wait()

    row_id = lax.broadcasted_iota(jnp.int32, (tokens, tokens), 0)
    col_id = lax.broadcasted_iota(jnp.int32, (tokens, tokens), 1)
    upper = (row_id <= col_id).astype(F32)
    lower = row_id >= col_id
    eye = (row_id == col_id).astype(F32)
    forget = forget_ref[...]
    run_row = dot(forget, upper, precision=HIGHEST)
    run_col = dot(lower.astype(F32), forget, ((1,), (1,)), precision=HIGHEST)
    gate_col = dot(eye, gate_ref[...], ((1,), (1,)), precision=HIGHEST)
    last = jnp.sum(forget, axis=1, keepdims=True)
    level[rank] = jnp.broadcast_to(last, (heads, dh))
    for p in others():
        pending.append(send(level.at[rank], level.at[rank], level_sems, p, rank, layer * ring + p))

    across = (rank + ring // 2) % ring
    sibling = rank + 1 - 2 * (rank % 2)
    sibling_id = layer * ring + sibling

    def to_sibling(index, part_side):
        piece = piece_of(weights, index, part_side)
        slot = index // ring * ring + index % ring // 2 * 2 + part_side
        pending.append(send(piece, piece, core_sems, slot, slot, sibling_id))

    def to_twin(index):
        piece = piece_of(weights, index, side)
        slot = index // ring * 2 + index % ring // 2
        pending.append(send(piece, piece, x_sems, slot, slot, me, twin))

    own = piece_of(w_ref, 0, side)
    landing = piece_of(weights, me, side)
    pending.append(send(own, landing, y_sems, layer, layer, layer * ring + across))
    for d in range(1, layers):
        there = (layer + d) % layers
        pending.append(send(own, landing, z_sems, there, layer, there * ring + rank))

    def from_column(d):
        there = (layer + d) % layers
        index = there * ring + rank
        piece = piece_of(weights, index, side)
        arrived(piece, z_sems, there)
        pending.append(send(piece, piece, y_sems, there, there, layer * ring + across))
        to_twin(index)
        to_sibling(index, side)

    def from_across(d):
        there = (layer + d) % layers
        index = there * ring + across
        arrived(piece_of(weights, index, side), y_sems, there)
        to_twin(index)
        to_sibling(index, side)

    def from_twin(d, place):
        there = (layer + d) % layers
        index = there * ring + place
        arrived(piece_of(weights, index, 1 - side), x_sems, there * 2 + place // 2)
        to_sibling(index, 1 - side)

    pre, keys_t, keys_low, beta_keys = [], [], [], []
    mixes, decays = [], []
    for h in range(heads):
        lanes = slice(h * dh, (h + 1) * dh)
        raw = k_ref[:, lanes]
        key = raw.astype(F32)
        scale = lax.rsqrt(jnp.sum(key * key, axis=1, keepdims=True) + EPS)
        beta = gate_col[:, h:h + 1]
        run = run_col[:, h:h + 1]
        tail = jnp.exp(last[h:h + 1, :] - run) * beta
        value = v_ref[:, lanes].astype(F32)
        unit = scale * key
        right = jnp.concatenate(
            [low((tail * scale) * unit), low((beta * scale) * unit), low((tail * scale) * value),
             low(scale * eye)], axis=1)
        made = dot(raw, right, ((0,), (0,)))
        gram_out[h] = low(made[:, :dh])
        pre.append(made[:, dh:2 * dh])
        state_out[h] = made[:, 2 * dh:3 * dh]
        keys_t.append(low(made[:, 3 * dh:]))
        beta_keys.append(low(beta * unit))
        mixes.append(jnp.where(lower, jnp.exp(jnp.minimum(run - run_row[h:h + 1, :], 0.0)), 0.0))
        decays.append(jnp.exp(run))

    mine = pl.ds(rank * share, share)
    kinds = (
        (gram_out, gram_in, gram_chain_in, gram_chain_out, gram_back, gram_full, 0),
        (state_out, state_in, state_chain_in, state_chain_out, state_back, state_full, 1),
    )

    def sems_of(sems, kind):
        return (sems[0].at[kind], sems[1].at[kind])

    for outgoing, incoming, *_, kind in kinds:
        for p in others():
            pending.append(send(
                outgoing.at[pl.ds(p * share, share)], incoming.at[rank],
                sems_of(piece_sems, kind), p, rank, layer * ring + p))
        incoming[rank] = outgoing[mine]
    loads[6].wait()
    to_sibling(me, side)
    to_sibling(me, 1 - side)

    for p in others():
        arrived(level.at[p], level_sems, p)
    chained = []

    def scan(outgoing, incoming, chain_in, chain_out, back, full, kind):
        for p in others():
            arrived(incoming.at[p], sems_of(piece_sems, kind), p)
        kept = incoming.dtype
        shrink, total = [], []
        for j in range(share):
            steps = [jnp.exp(level[p, pl.ds(rank * share + j, 1), :]) for p in range(ring)]
            whole = jnp.zeros((dh, dh), F32)
            for p in range(ring):
                whole = steps[p] * whole + incoming[p, j].astype(F32)
            shrink.append(steps)
            total.append(whole)

        @pl.when(layer == 0)
        def _():
            chain_in[...] = jnp.zeros_like(chain_in)

        for j in range(share):
            @pl.when(layer > 0)
            def _():
                arrived(chain_in.at[j], sems_of(chain_sems, kind), j)

            @pl.when(layer < layers - 1)
            def _():
                steps = shrink[j]
                over = steps[0]
                for p in range(1, ring):
                    over = over * steps[p]
                chain_out[j] = (over * chain_in[j].astype(F32) + total[j]).astype(kept)
                send(chain_out.at[j], chain_in.at[j], sems_of(chain_sems, kind), j, j, me + ring)
        for j in range(share):
            current = chain_in[j].astype(F32)
            for p in range(ring):
                back[p, j] = current.astype(kept)
                if p < ring - 1:
                    current = shrink[j][p] * current + incoming[p, j].astype(F32)
        for p in others():
            pending.append(send(back.at[p], full.at[mine], sems_of(back_sems, kind), p, rank, layer * ring + p))
        full[mine] = back[rank]
        chained.append((chain_out, chain_in, kind))

    scan(*kinds[0])
    scan(*kinds[1])
    for p in others():
        arrived(gram_full.at[pl.ds(p * share, share)], sems_of(back_sems, 0), p)
    from_across(0)
    for d in range(1, layers - 1):
        from_column(d)

    starts = [gram_full[h] for h in range(heads)]
    systems, inverses, bounds = [], [], []
    for h in range(heads):
        system = starts[h].astype(F32) + pre[h] + ridge_ref[h] * eye
        bound = jnp.max(jnp.sum(jnp.abs(system), axis=0, keepdims=True), axis=1, keepdims=True)
        inv = 1.0 / bound
        inverses.append(low((2.0 * eye - system * inv) * inv))
        systems.append(low(system))
    for step in range(NEWTON - 1):
        rests = [low(2.0 * eye - dot(systems[h], inverses[h])) for h in range(heads)]
        inverses = [low(dot(inverses[h], rests[h])) for h in range(heads)]
    if layers > 1:
        from_column(layers - 1)
    loads[4].wait()
    loads[5].wait()

    both = [jnp.concatenate([starts[h], keys_t[h]], axis=1) for h in range(heads)]
    queries, solved = [], []
    for h in range(heads):
        query = q_ref[:, h * dh:(h + 1) * dh].astype(F32)
        query = query * lax.rsqrt(jnp.sum(query * query, axis=1, keepdims=True) + EPS)
        queries.append(query)
        solved.append(dot(low(query), inverses[h]))
    for step in range(CORR - 1):
        for h in range(heads):
            joint = dot(low(solved[h]), both[h])
            applied = (
                decays[h] * joint[:, :dh]
                + dot(low(mixes[h] * joint[:, dh:]), beta_keys[h])
                + ridge_ref[h] * solved[h]
            )
            solved[h] = solved[h] + dot(low(queries[h] - applied), inverses[h])
        if step == 0:
            for d in range(1, layers - 1):
                from_across(d)
            for d in range(1, layers - 1):
                from_twin(d, rank)
        if step == 1:
            if layers > 1:
                from_across(layers - 1)
                from_twin(layers - 1, rank)
            from_twin(0, across)
    for d in range(1, layers):
        from_twin(d, across)

    for p in others():
        arrived(state_full.at[pl.ds(p * share, share)], sems_of(back_sems, 1), p)
    for h in range(heads):
        lanes = slice(h * dh, (h + 1) * dh)
        scores = mixes[h] * split_dot(solved[h], keys_t[h])
        value = low(gate_col[:, h:h + 1] * v_ref[:, lanes].astype(F32))
        state = state_full[h]
        output = decays[h] * split_dot(solved[h], low(state)) + dot(low(scores), value)
        output = output + decays[h] * dot(low(solved[h]), low(state - low(state).astype(F32)))
        norm = lax.rsqrt(jnp.mean(output * output, axis=1, keepdims=True) + EPS)
        y_ref[:, lanes] = low(output * norm * gain_ref[:, lanes])

    for there in range(layers):
        for i in range(ring // 2):
            for part_side in range(2):
                index = there * ring + i * 2 + sibling % 2
                arrived(piece_of(weights, index, part_side), core_sems, there * ring + i * 2 + part_side)
    width = min(512, columns)
    for c in range(0, columns, width):
        out_ref[:, c:c + width] = low(dot(y_ref[...], weights[:, c:c + width]))

    for copy in pending:
        copy.wait_send()
    for chain_out, chain_in, kind in chained:
        @pl.when(layer < layers - 1)
        def _():
            for j in range(share):
                sems = sems_of(chain_sems, kind)
                pltpu.make_async_remote_copy(
                    src_ref=chain_out.at[j], dst_ref=chain_in.at[j], send_sem=sems[0].at[j],
                    recv_sem=sems[1].at[j], device_id={"seq": me + ring}, device_id_type=MESH,
                ).wait_send()


def wrapped(body, *refs):
    tail = refs[-16:]
    pairs = [(tail[i], tail[i + 1]) for i in range(0, 16, 2)]
    body(*refs[:-16], *pairs)


def solution(mesh):
    n = mesh.shape["seq"]
    ring = 4
    layers = n // ring

    def on_device(queries, keys, values, log_forget, input_gate, ridge, gain, out_weight):
        tokens, features = queries.shape
        heads = log_forget.shape[0]
        dh = features // heads
        share = heads // ring
        rows, columns = out_weight.shape

        def scans(kind):
            return [
                pltpu.VMEM((heads, dh, dh), kind),
                pltpu.VMEM((ring, share, dh, dh), kind),
                pltpu.VMEM((share, dh, dh), kind),
                pltpu.VMEM((share, dh, dh), kind),
                pltpu.VMEM((ring, share, dh, dh), kind),
                pltpu.VMEM((heads, dh, dh), kind),
            ]

        def pair(*shape):
            return [pltpu.SemaphoreType.DMA(shape), pltpu.SemaphoreType.DMA(shape)]

        vmem = pl.BlockSpec(memory_space=pltpu.VMEM)
        hbm = pl.BlockSpec(memory_space=pltpu.HBM)
        smem = pl.BlockSpec(memory_space=pltpu.SMEM)
        return pl.pallas_call(
            functools.partial(wrapped, functools.partial(kernel, layers, ring, heads)),
            out_shape=jax.ShapeDtypeStruct((tokens, columns), BF16),
            in_specs=[hbm, hbm, hbm, hbm, hbm, smem, hbm, hbm],
            out_specs=vmem,
            scratch_shapes=[
                pltpu.VMEM((tokens, features), BF16),
                pltpu.VMEM((tokens, features), BF16),
                pltpu.VMEM((tokens, features), BF16),
                pltpu.VMEM((heads, tokens), F32),
                pltpu.VMEM((heads, tokens), F32),
                pltpu.VMEM((1, features), F32),
                pltpu.SemaphoreType.DMA((7,)),
                pltpu.VMEM((ring, heads, dh), F32),
                *scans(BF16),
                *scans(F32),
                pltpu.VMEM((n * rows, columns), BF16),
                pltpu.VMEM((tokens, features), BF16),
                *pair(ring),
                *pair(2, ring),
                *pair(2, share),
                *pair(2, ring),
                *pair(layers),
                *pair(layers),
                *pair(layers * 2),
                *pair(layers * ring),
            ],
            compiler_params=pltpu.CompilerParams(
                collective_id=0, has_side_effects=True, vmem_limit_bytes=56 * 1024 * 1024),
        )(queries, keys, values, log_forget, input_gate, ridge, gain.reshape(1, features), out_weight)

    placed = (
        P(("parts", "seq"), None),
        P(("parts", "seq"), None),
        P(("parts", "seq"), None),
        P(None, ("parts", "seq")),
        P(None, ("parts", "seq")),
        P(),
        P(),
        P("seq", None),
    )
    return jax.shard_map(
        on_device, mesh=mesh, in_specs=placed, out_specs=P(("parts", "seq"), None), check_vma=False
    )
```

```python
import functools

import jax
import jax.numpy as jnp
from jax import lax
from jax.experimental import pallas as pl
from jax.experimental.pallas import tpu as pltpu
from jax.sharding import PartitionSpec as P

NEWTON = 6
CORR = 4
EPS = 1e-06
F32 = jnp.float32
BF16 = jnp.bfloat16
MESH = pl.DeviceIdType.MESH
HIGHEST = lax.Precision.HIGHEST


def dot(a, b, dims=((1,), (0,)), precision=None):
    return lax.dot_general(a, b, (dims, ((), ())), precision=precision, preferred_element_type=F32)


def low(a):
    return a.astype(BF16)


def kernel(
    layers, ring, heads, q_hbm, k_hbm, v_hbm, forget_hbm, gate_hbm, ridge_ref, gain_hbm, w_ref,
    out_ref, q_ref, k_ref, v_ref, forget_ref, gate_ref, gain_ref, load_sems, level, gram_out, gram_in, gram_chain_in, gram_chain_out, gram_back, gram_full,
    state_out, state_in, state_chain_in, state_chain_out, state_back, state_full,
    weights, y_ref,
    level_sems, piece_sems, chain_sems, back_sems, z_sems, y_sems, x_sems, core_sems,
):
    me = lax.axis_index("seq")
    layer, rank = me // ring, me % ring
    share = heads // ring
    tokens = q_ref.shape[0]
    dh = q_ref.shape[1] // heads
    rows, columns = w_ref.shape
    half = columns // 2
    part = lax.axis_index("parts")
    side = part % 2
    twin = part + 1 - 2 * side
    pending = []

    def others():
        return [(rank + d) % ring for d in range(1, ring)]

    def send(src, dst, sems, slot_out, slot_in, target, where=None):
        copy = pltpu.make_async_remote_copy(
            src_ref=src, dst_ref=dst, send_sem=sems[0].at[slot_out], recv_sem=sems[1].at[slot_in],
            device_id={"seq": target} if where is None else {"parts": where, "seq": target},
            device_id_type=MESH,
        )
        copy.start()
        return copy

    def arrived(dst, sems, slot):
        pltpu.make_async_remote_copy(
            src_ref=dst, dst_ref=dst, send_sem=sems[0].at[slot], recv_sem=sems[1].at[slot],
            device_id={"seq": (me + 1) % (layers * ring)}, device_id_type=MESH,
        ).wait_recv()

    def piece_of(ref, index, part_side):
        return ref.at[pl.ds(pl.multiple_of(index * rows, rows), rows),
                      pl.ds(pl.multiple_of(part_side * half, 128), half)]

    loads = []
    for i, (src, dst) in enumerate((
        (forget_hbm, forget_ref), (gate_hbm, gate_ref), (k_hbm, k_ref), (v_hbm, v_ref), (q_hbm, q_ref),
        (gain_hbm, gain_ref), (w_ref, weights.at[pl.ds(pl.multiple_of(me * rows, rows), rows)]),
    )):
        loads.append(pltpu.make_async_copy(src, dst, load_sems.at[i]))
        loads[-1].start()

    barrier = pltpu.get_barrier_semaphore()
    partners = [layer * ring + p for p in others()]
    partners += [((layer + d) % layers) * ring + rank for d in range(1, layers)]
    for partner in partners:
        pl.semaphore_signal(barrier, inc=1, device_id={"seq": partner}, device_id_type=MESH)
    pl.semaphore_signal(
        barrier, inc=1, device_id={"parts": twin, "seq": me}, device_id_type=MESH)
    pl.semaphore_wait(barrier, len(partners) + 1)
    for load in loads[:4]:
        load.wait()

    row_id = lax.broadcasted_iota(jnp.int32, (tokens, tokens), 0)
    col_id = lax.broadcasted_iota(jnp.int32, (tokens, tokens), 1)
    upper = (row_id <= col_id).astype(F32)
    lower = row_id >= col_id
    eye = (row_id == col_id).astype(F32)
    forget = forget_ref[...]
    run_row = dot(forget, upper, precision=HIGHEST)
    run_col = dot(lower.astype(F32), forget, ((1,), (1,)), precision=HIGHEST)
    gate_col = dot(eye, gate_ref[...], ((1,), (1,)), precision=HIGHEST)
    last = jnp.sum(forget, axis=1, keepdims=True)
    level[rank] = jnp.broadcast_to(last, (heads, dh))
    for p in others():
        pending.append(send(level.at[rank], level.at[rank], level_sems, p, rank, layer * ring + p))

    across = (rank + ring // 2) % ring
    sibling = rank + 1 - 2 * (rank % 2)
    sibling_id = layer * ring + sibling

    def to_sibling(index, part_side):
        piece = piece_of(weights, index, part_side)
        slot = index // ring * ring + index % ring // 2 * 2 + part_side
        pending.append(send(piece, piece, core_sems, slot, slot, sibling_id))

    def to_twin(index):
        piece = piece_of(weights, index, side)
        slot = index // ring * 2 + index % ring // 2
        pending.append(send(piece, piece, x_sems, slot, slot, me, twin))

    own = piece_of(w_ref, 0, side)
    landing = piece_of(weights, me, side)
    pending.append(send(own, landing, y_sems, layer, layer, layer * ring + across))
    for d in range(1, layers):
        there = (layer + d) % layers
        pending.append(send(own, landing, z_sems, there, layer, there * ring + rank))

    def from_column(d):
        there = (layer + d) % layers
        index = there * ring + rank
        piece = piece_of(weights, index, side)
        arrived(piece, z_sems, there)
        pending.append(send(piece, piece, y_sems, there, there, layer * ring + across))
        to_twin(index)
        to_sibling(index, side)

    def from_across(d):
        there = (layer + d) % layers
        index = there * ring + across
        arrived(piece_of(weights, index, side), y_sems, there)
        to_twin(index)
        to_sibling(index, side)

    def from_twin(d, place):
        there = (layer + d) % layers
        index = there * ring + place
        arrived(piece_of(weights, index, 1 - side), x_sems, there * 2 + place // 2)
        to_sibling(index, 1 - side)

    pre, keys_t, keys_low, beta_keys = [], [], [], []
    mixes, decays = [], []
    for h in range(heads):
        lanes = slice(h * dh, (h + 1) * dh)
        raw = k_ref[:, lanes]
        key = raw.astype(F32)
        scale = lax.rsqrt(jnp.sum(key * key, axis=1, keepdims=True) + EPS)
        beta = gate_col[:, h:h + 1]
        run = run_col[:, h:h + 1]
        tail = jnp.exp(last[h:h + 1, :] - run) * beta
        value = v_ref[:, lanes].astype(F32)
        unit = scale * key
        right = jnp.concatenate(
            [low((tail * scale) * unit), low((beta * scale) * unit), low((tail * scale) * value),
             low(scale * eye)], axis=1)
        made = dot(raw, right, ((0,), (0,)))
        gram_out[h] = low(made[:, :dh])
        pre.append(made[:, dh:2 * dh])
        state_out[h] = made[:, 2 * dh:3 * dh]
        keys_t.append(low(made[:, 3 * dh:]))
        beta_keys.append(low(beta * unit))
        mixes.append(jnp.where(lower, jnp.exp(jnp.minimum(run - run_row[h:h + 1, :], 0.0)), 0.0))
        decays.append(jnp.exp(run))

    mine = pl.ds(rank * share, share)
    kinds = (
        (gram_out, gram_in, gram_chain_in, gram_chain_out, gram_back, gram_full, 0),
        (state_out, state_in, state_chain_in, state_chain_out, state_back, state_full, 1),
    )

    def sems_of(sems, kind):
        return (sems[0].at[kind], sems[1].at[kind])

    def exchange(outgoing, incoming, *_):
        kind = _[-1]
        for p in others():
            pending.append(send(
                outgoing.at[pl.ds(p * share, share)], incoming.at[rank],
                sems_of(piece_sems, kind), p, rank, layer * ring + p))
        incoming[rank] = outgoing[mine]

    exchange(*kinds[0])
    loads[6].wait()
    to_sibling(me, side)
    to_sibling(me, 1 - side)

    for p in others():
        arrived(level.at[p], level_sems, p)
    chained = []

    def scan(outgoing, incoming, chain_in, chain_out, back, full, kind):
        for p in others():
            arrived(incoming.at[p], sems_of(piece_sems, kind), p)
        kept = incoming.dtype
        shrink, total = [], []
        for j in range(share):
            steps = [jnp.exp(level[p, pl.ds(rank * share + j, 1), :]) for p in range(ring)]
            whole = jnp.zeros((dh, dh), F32)
            for p in range(ring):
                whole = steps[p] * whole + incoming[p, j].astype(F32)
            shrink.append(steps)
            total.append(whole)

        @pl.when(layer == 0)
        def _():
            chain_in[...] = jnp.zeros_like(chain_in)

        for j in range(share):
            @pl.when(layer > 0)
            def _():
                arrived(chain_in.at[j], sems_of(chain_sems, kind), j)

            @pl.when(layer < layers - 1)
            def _():
                steps = shrink[j]
                over = steps[0]
                for p in range(1, ring):
                    over = over * steps[p]
                chain_out[j] = (over * chain_in[j].astype(F32) + total[j]).astype(kept)
                send(chain_out.at[j], chain_in.at[j], sems_of(chain_sems, kind), j, j, me + ring)
        for j in range(share):
            current = chain_in[j].astype(F32)
            for p in range(ring):
                back[p, j] = current.astype(kept)
                if p < ring - 1:
                    current = shrink[j][p] * current + incoming[p, j].astype(F32)
        for p in others():
            pending.append(send(back.at[p], full.at[mine], sems_of(back_sems, kind), p, rank, layer * ring + p))
        full[mine] = back[rank]
        chained.append((chain_out, chain_in, kind))

    scan(*kinds[0])
    exchange(*kinds[1])
    for p in others():
        arrived(gram_full.at[pl.ds(p * share, share)], sems_of(back_sems, 0), p)
    starts = [gram_full[h] for h in range(heads)]
    systems, inverses, bounds = [], [], []
    for h in range(heads):
        system = starts[h].astype(F32) + pre[h] + ridge_ref[h] * eye
        bound = jnp.max(jnp.sum(jnp.abs(system), axis=0, keepdims=True), axis=1, keepdims=True)
        inv = 1.0 / bound
        inverses.append(low((2.0 * eye - system * inv) * inv))
        systems.append(low(system))
    for step in range(NEWTON - 1):
        rests = [low(2.0 * eye - dot(systems[h], inverses[h])) for h in range(heads)]
        inverses = [low(dot(inverses[h], rests[h])) for h in range(heads)]
        if step == 0:
            from_across(0)
            for d in range(1, layers - 1):
                from_column(d)
        if step == 2:
            scan(*kinds[1])
    if layers > 1:
        from_column(layers - 1)
    loads[4].wait()
    loads[5].wait()

    both = [jnp.concatenate([starts[h], keys_t[h]], axis=1) for h in range(heads)]
    queries, solved = [], []
    for h in range(heads):
        query = q_ref[:, h * dh:(h + 1) * dh].astype(F32)
        query = query * lax.rsqrt(jnp.sum(query * query, axis=1, keepdims=True) + EPS)
        queries.append(query)
        solved.append(dot(low(query), inverses[h]))
    for step in range(CORR - 1):
        joints = [dot(low(solved[h]), both[h]) for h in range(heads)]
        mixed = [dot(low(mixes[h] * joints[h][:, dh:]), beta_keys[h]) for h in range(heads)]
        rests = [
            low(queries[h] - (decays[h] * joints[h][:, :dh] + mixed[h] + ridge_ref[h] * solved[h]))
            for h in range(heads)
        ]
        solved = [solved[h] + dot(rests[h], inverses[h]) for h in range(heads)]
        if step == 0:
            for d in range(1, layers - 1):
                from_across(d)
            for d in range(1, layers - 1):
                from_twin(d, rank)
        if step == 1:
            if layers > 1:
                from_across(layers - 1)
                from_twin(layers - 1, rank)
            from_twin(0, across)
    for d in range(1, layers):
        from_twin(d, across)

    for p in others():
        arrived(state_full.at[pl.ds(p * share, share)], sems_of(back_sems, 1), p)
    joints, scores = [], []
    for h in range(heads):
        state = state_full[h]
        near = low(state)
        high = low(solved[h])
        right = jnp.concatenate([near, keys_t[h]], axis=1)
        joint = dot(high, right) + dot(low(solved[h] - high.astype(F32)), right)
        joints.append(joint[:, :dh] + dot(high, low(state - near.astype(F32))))
        scores.append(low(mixes[h] * joint[:, dh:]))
    for h in range(heads):
        lanes = slice(h * dh, (h + 1) * dh)
        value = low(gate_col[:, h:h + 1] * v_ref[:, lanes].astype(F32))
        output = decays[h] * joints[h] + dot(scores[h], value)
        norm = lax.rsqrt(jnp.mean(output * output, axis=1, keepdims=True) + EPS)
        y_ref[:, lanes] = low(output * norm * gain_ref[:, lanes])

    for there in range(layers):
        for i in range(ring // 2):
            for part_side in range(2):
                index = there * ring + i * 2 + sibling % 2
                arrived(piece_of(weights, index, part_side), core_sems, there * ring + i * 2 + part_side)
    width = min(512, columns)
    for c in range(0, columns, width):
        out_ref[:, c:c + width] = low(dot(y_ref[...], weights[:, c:c + width]))

    for copy in pending:
        copy.wait_send()
    for chain_out, chain_in, kind in chained:
        @pl.when(layer < layers - 1)
        def _():
            for j in range(share):
                sems = sems_of(chain_sems, kind)
                pltpu.make_async_remote_copy(
                    src_ref=chain_out.at[j], dst_ref=chain_in.at[j], send_sem=sems[0].at[j],
                    recv_sem=sems[1].at[j], device_id={"seq": me + ring}, device_id_type=MESH,
                ).wait_send()


def wrapped(body, *refs):
    tail = refs[-16:]
    pairs = [(tail[i], tail[i + 1]) for i in range(0, 16, 2)]
    body(*refs[:-16], *pairs)


def solution(mesh):
    n = mesh.shape["seq"]
    ring = 4
    layers = n // ring

    def on_device(queries, keys, values, log_forget, input_gate, ridge, gain, out_weight):
        tokens, features = queries.shape
        heads = log_forget.shape[0]
        dh = features // heads
        share = heads // ring
        rows, columns = out_weight.shape

        def scans(kind):
            return [
                pltpu.VMEM((heads, dh, dh), kind),
                pltpu.VMEM((ring, share, dh, dh), kind),
                pltpu.VMEM((share, dh, dh), kind),
                pltpu.VMEM((share, dh, dh), kind),
                pltpu.VMEM((ring, share, dh, dh), kind),
                pltpu.VMEM((heads, dh, dh), kind),
            ]

        def pair(*shape):
            return [pltpu.SemaphoreType.DMA(shape), pltpu.SemaphoreType.DMA(shape)]

        vmem = pl.BlockSpec(memory_space=pltpu.VMEM)
        hbm = pl.BlockSpec(memory_space=pltpu.HBM)
        smem = pl.BlockSpec(memory_space=pltpu.SMEM)
        return pl.pallas_call(
            functools.partial(wrapped, functools.partial(kernel, layers, ring, heads)),
            out_shape=jax.ShapeDtypeStruct((tokens, columns), BF16),
            in_specs=[hbm, hbm, hbm, hbm, hbm, smem, hbm, hbm],
            out_specs=vmem,
            scratch_shapes=[
                pltpu.VMEM((tokens, features), BF16),
                pltpu.VMEM((tokens, features), BF16),
                pltpu.VMEM((tokens, features), BF16),
                pltpu.VMEM((heads, tokens), F32),
                pltpu.VMEM((heads, tokens), F32),
                pltpu.VMEM((1, features), F32),
                pltpu.SemaphoreType.DMA((7,)),
                pltpu.VMEM((ring, heads, dh), F32),
                *scans(BF16),
                *scans(F32),
                pltpu.VMEM((n * rows, columns), BF16),
                pltpu.VMEM((tokens, features), BF16),
                *pair(ring),
                *pair(2, ring),
                *pair(2, share),
                *pair(2, ring),
                *pair(layers),
                *pair(layers),
                *pair(layers * 2),
                *pair(layers * ring),
            ],
            compiler_params=pltpu.CompilerParams(
                collective_id=0, has_side_effects=True, vmem_limit_bytes=56 * 1024 * 1024),
        )(queries, keys, values, log_forget, input_gate, ridge, gain.reshape(1, features), out_weight)

    placed = (
        P(("parts", "seq"), None),
        P(("parts", "seq"), None),
        P(("parts", "seq"), None),
        P(None, ("parts", "seq")),
        P(None, ("parts", "seq")),
        P(),
        P(),
        P("seq", None),
    )
    return jax.shard_map(
        on_device, mesh=mesh, in_specs=placed, out_specs=P(("parts", "seq"), None), check_vma=False
    )
```

```python
import functools

import jax
import jax.numpy as jnp
from jax import lax
from jax.experimental import pallas as pl
from jax.experimental.pallas import tpu as pltpu
from jax.sharding import PartitionSpec as P

NEWTON = 6
CORR = 4
EPS = 1e-06
F32 = jnp.float32
BF16 = jnp.bfloat16
MESH = pl.DeviceIdType.MESH
HIGHEST = lax.Precision.HIGHEST


def dot(a, b, dims=((1,), (0,)), precision=None):
    return lax.dot_general(a, b, (dims, ((), ())), precision=precision, preferred_element_type=F32)


def low(a):
    return a.astype(BF16)


def kernel(
    layers, ring, heads, q_hbm, k_hbm, v_hbm, forget_hbm, gate_hbm, ridge_ref, gain_hbm, w_ref,
    out_ref, q_ref, k_ref, v_ref, forget_ref, gate_ref, gain_ref, load_sems, level, gram_out, gram_in, gram_chain_in, gram_chain_out, gram_back, gram_full,
    state_out, state_in, state_chain_in, state_chain_out, state_back, state_full,
    weights, y_ref,
    level_sems, piece_sems, chain_sems, back_sems, z_sems, y_sems, x_sems, core_sems,
):
    me = lax.axis_index("seq")
    layer, rank = me // ring, me % ring
    share = heads // ring
    tokens = q_ref.shape[0]
    dh = q_ref.shape[1] // heads
    rows, columns = w_ref.shape
    half = columns // 2
    part = lax.axis_index("parts")
    side = part % 2
    twin = part + 1 - 2 * side
    pending = []

    def others():
        return [(rank + d) % ring for d in range(1, ring)]

    def send(src, dst, sems, slot_out, slot_in, target, where=None):
        copy = pltpu.make_async_remote_copy(
            src_ref=src, dst_ref=dst, send_sem=sems[0].at[slot_out], recv_sem=sems[1].at[slot_in],
            device_id={"seq": target} if where is None else {"parts": where, "seq": target},
            device_id_type=MESH,
        )
        copy.start()
        return copy

    def arrived(dst, sems, slot):
        pltpu.make_async_remote_copy(
            src_ref=dst, dst_ref=dst, send_sem=sems[0].at[slot], recv_sem=sems[1].at[slot],
            device_id={"seq": (me + 1) % (layers * ring)}, device_id_type=MESH,
        ).wait_recv()

    def piece_of(ref, index, part_side):
        return ref.at[pl.ds(pl.multiple_of(index * rows, rows), rows),
                      pl.ds(pl.multiple_of(part_side * half, 128), half)]

    loads = []
    for i, (src, dst) in enumerate((
        (forget_hbm, forget_ref), (gate_hbm, gate_ref), (k_hbm, k_ref), (v_hbm, v_ref), (q_hbm, q_ref),
        (gain_hbm, gain_ref), (w_ref, weights.at[pl.ds(pl.multiple_of(me * rows, rows), rows)]),
    )):
        loads.append(pltpu.make_async_copy(src, dst, load_sems.at[i]))
        loads[-1].start()

    barrier = pltpu.get_barrier_semaphore()
    partners = [layer * ring + p for p in others()]
    partners += [((layer + d) % layers) * ring + rank for d in range(1, layers)]
    for partner in partners:
        pl.semaphore_signal(barrier, inc=1, device_id={"seq": partner}, device_id_type=MESH)
    pl.semaphore_signal(
        barrier, inc=1, device_id={"parts": twin, "seq": me}, device_id_type=MESH)
    pl.semaphore_wait(barrier, len(partners) + 1)
    for load in loads[:4]:
        load.wait()

    row_id = lax.broadcasted_iota(jnp.int32, (tokens, tokens), 0)
    col_id = lax.broadcasted_iota(jnp.int32, (tokens, tokens), 1)
    upper = (row_id <= col_id).astype(F32)
    lower = row_id >= col_id
    eye = (row_id == col_id).astype(F32)
    forget = forget_ref[...]
    run_row = dot(forget, upper, precision=HIGHEST)
    run_col = dot(lower.astype(F32), forget, ((1,), (1,)), precision=HIGHEST)
    gate_col = dot(eye, gate_ref[...], ((1,), (1,)), precision=HIGHEST)
    last = jnp.sum(forget, axis=1, keepdims=True)
    level[rank] = jnp.broadcast_to(last, (heads, dh))
    for p in others():
        pending.append(send(level.at[rank], level.at[rank], level_sems, p, rank, layer * ring + p))

    across = (rank + ring // 2) % ring
    sibling = rank + 1 - 2 * (rank % 2)
    sibling_id = layer * ring + sibling

    def to_sibling(index, part_side):
        piece = piece_of(weights, index, part_side)
        slot = index // ring * ring + index % ring // 2 * 2 + part_side
        pending.append(send(piece, piece, core_sems, slot, slot, sibling_id))

    def to_twin(index):
        piece = piece_of(weights, index, side)
        slot = index // ring * 2 + index % ring // 2
        pending.append(send(piece, piece, x_sems, slot, slot, me, twin))

    own = piece_of(w_ref, 0, side)
    landing = piece_of(weights, me, side)
    pending.append(send(own, landing, y_sems, layer, layer, layer * ring + across))
    for d in range(1, layers):
        there = (layer + d) % layers
        pending.append(send(own, landing, z_sems, there, layer, there * ring + rank))

    def from_column(d):
        there = (layer + d) % layers
        index = there * ring + rank
        piece = piece_of(weights, index, side)
        arrived(piece, z_sems, there)
        pending.append(send(piece, piece, y_sems, there, there, layer * ring + across))
        to_twin(index)
        to_sibling(index, side)

    def from_across(d):
        there = (layer + d) % layers
        index = there * ring + across
        arrived(piece_of(weights, index, side), y_sems, there)
        to_twin(index)
        to_sibling(index, side)

    def from_twin(d, place):
        there = (layer + d) % layers
        index = there * ring + place
        arrived(piece_of(weights, index, 1 - side), x_sems, there * 2 + place // 2)
        to_sibling(index, 1 - side)

    pre, keys_t, keys_low, beta_keys = [], [], [], []
    mixes, decays = [], []
    for h in range(heads):
        lanes = slice(h * dh, (h + 1) * dh)
        raw = k_ref[:, lanes]
        key = raw.astype(F32)
        scale = lax.rsqrt(jnp.sum(key * key, axis=1, keepdims=True) + EPS)
        beta = gate_col[:, h:h + 1]
        run = run_col[:, h:h + 1]
        tail = jnp.exp(last[h:h + 1, :] - run) * beta
        value = v_ref[:, lanes].astype(F32)
        unit = scale * key
        right = jnp.concatenate(
            [low((tail * scale) * unit), low((beta * scale) * unit), low((tail * scale) * value),
             low(scale * eye)], axis=1)
        made = dot(raw, right, ((0,), (0,)))
        gram_out[h] = low(made[:, :dh])
        pre.append(made[:, dh:2 * dh])
        state_out[h] = low(made[:, 2 * dh:3 * dh])
        keys_t.append(low(made[:, 3 * dh:]))
        beta_keys.append(low(beta * unit))
        mixes.append(jnp.where(lower, jnp.exp(jnp.minimum(run - run_row[h:h + 1, :], 0.0)), 0.0))
        decays.append(jnp.exp(run))

    mine = pl.ds(rank * share, share)
    kinds = (
        (gram_out, gram_in, gram_chain_in, gram_chain_out, gram_back, gram_full, 0),
        (state_out, state_in, state_chain_in, state_chain_out, state_back, state_full, 1),
    )

    def sems_of(sems, kind):
        return (sems[0].at[kind], sems[1].at[kind])

    def exchange(outgoing, incoming, *_):
        kind = _[-1]
        for p in others():
            pending.append(send(
                outgoing.at[pl.ds(p * share, share)], incoming.at[rank],
                sems_of(piece_sems, kind), p, rank, layer * ring + p))
        incoming[rank] = outgoing[mine]

    exchange(*kinds[0])
    loads[6].wait()
    to_sibling(me, side)
    to_sibling(me, 1 - side)

    for p in others():
        arrived(level.at[p], level_sems, p)
    chained = []

    def scan(outgoing, incoming, chain_in, chain_out, back, full, kind):
        for p in others():
            arrived(incoming.at[p], sems_of(piece_sems, kind), p)
        kept = incoming.dtype
        shrink, total = [], []
        for j in range(share):
            steps = [jnp.exp(level[p, pl.ds(rank * share + j, 1), :]) for p in range(ring)]
            whole = jnp.zeros((dh, dh), F32)
            for p in range(ring):
                whole = steps[p] * whole + incoming[p, j].astype(F32)
            shrink.append(steps)
            total.append(whole)

        @pl.when(layer == 0)
        def _():
            chain_in[...] = jnp.zeros_like(chain_in)

        for j in range(share):
            @pl.when(layer > 0)
            def _():
                arrived(chain_in.at[j], sems_of(chain_sems, kind), j)

            @pl.when(layer < layers - 1)
            def _():
                steps = shrink[j]
                over = steps[0]
                for p in range(1, ring):
                    over = over * steps[p]
                chain_out[j] = (over * chain_in[j].astype(F32) + total[j]).astype(kept)
                send(chain_out.at[j], chain_in.at[j], sems_of(chain_sems, kind), j, j, me + ring)
        for j in range(share):
            current = chain_in[j].astype(F32)
            for p in range(ring):
                back[p, j] = current.astype(kept)
                if p < ring - 1:
                    current = shrink[j][p] * current + incoming[p, j].astype(F32)
        for p in others():
            pending.append(send(back.at[p], full.at[mine], sems_of(back_sems, kind), p, rank, layer * ring + p))
        full[mine] = back[rank]
        chained.append((chain_out, chain_in, kind))

    scan(*kinds[0])
    exchange(*kinds[1])
    for p in others():
        arrived(gram_full.at[pl.ds(p * share, share)], sems_of(back_sems, 0), p)
    starts = [gram_full[h] for h in range(heads)]
    systems, inverses, bounds = [], [], []
    for h in range(heads):
        system = starts[h].astype(F32) + pre[h] + ridge_ref[h] * eye
        bound = jnp.max(jnp.sum(jnp.abs(system), axis=0, keepdims=True), axis=1, keepdims=True)
        inv = 1.0 / bound
        inverses.append(low((2.0 * eye - system * inv) * inv))
        systems.append(low(system))
    for step in range(NEWTON - 1):
        rests = [low(2.0 * eye - dot(systems[h], inverses[h])) for h in range(heads)]
        inverses = [low(dot(inverses[h], rests[h])) for h in range(heads)]
        if step == 0:
            from_across(0)
            for d in range(1, layers - 1):
                from_column(d)
        if step == 2:
            scan(*kinds[1])
    if layers > 1:
        from_column(layers - 1)
    loads[4].wait()
    loads[5].wait()

    both = [jnp.concatenate([starts[h], keys_t[h]], axis=1) for h in range(heads)]
    queries, solved = [], []
    for h in range(heads):
        query = q_ref[:, h * dh:(h + 1) * dh].astype(F32)
        query = query * lax.rsqrt(jnp.sum(query * query, axis=1, keepdims=True) + EPS)
        queries.append(query)
        solved.append(dot(low(query), inverses[h]))
    for step in range(CORR - 1):
        joints = [dot(low(solved[h]), both[h]) for h in range(heads)]
        mixed = [dot(low(mixes[h] * joints[h][:, dh:]), beta_keys[h]) for h in range(heads)]
        rests = [
            low(queries[h] - (decays[h] * joints[h][:, :dh] + mixed[h] + ridge_ref[h] * solved[h]))
            for h in range(heads)
        ]
        solved = [solved[h] + dot(rests[h], inverses[h]) for h in range(heads)]
        if step == 0:
            for d in range(1, layers - 1):
                from_across(d)
            for d in range(1, layers - 1):
                from_twin(d, rank)
        if step == 1:
            if layers > 1:
                from_across(layers - 1)
                from_twin(layers - 1, rank)
            from_twin(0, across)
    for d in range(1, layers):
        from_twin(d, across)

    for p in others():
        arrived(state_full.at[pl.ds(p * share, share)], sems_of(back_sems, 1), p)
    joints, scores = [], []
    for h in range(heads):
        near = state_full[h]
        high = low(solved[h])
        right = jnp.concatenate([near, keys_t[h]], axis=1)
        joint = dot(high, right) + dot(low(solved[h] - high.astype(F32)), right)
        joints.append(joint[:, :dh])
        scores.append(low(mixes[h] * joint[:, dh:]))
    for h in range(heads):
        lanes = slice(h * dh, (h + 1) * dh)
        value = low(gate_col[:, h:h + 1] * v_ref[:, lanes].astype(F32))
        output = decays[h] * joints[h] + dot(scores[h], value)
        norm = lax.rsqrt(jnp.mean(output * output, axis=1, keepdims=True) + EPS)
        y_ref[:, lanes] = low(output * norm * gain_ref[:, lanes])

    for there in range(layers):
        for i in range(ring // 2):
            for part_side in range(2):
                index = there * ring + i * 2 + sibling % 2
                arrived(piece_of(weights, index, part_side), core_sems, there * ring + i * 2 + part_side)
    width = min(512, columns)
    for c in range(0, columns, width):
        out_ref[:, c:c + width] = low(dot(y_ref[...], weights[:, c:c + width]))

    for copy in pending:
        copy.wait_send()
    for chain_out, chain_in, kind in chained:
        @pl.when(layer < layers - 1)
        def _():
            for j in range(share):
                sems = sems_of(chain_sems, kind)
                pltpu.make_async_remote_copy(
                    src_ref=chain_out.at[j], dst_ref=chain_in.at[j], send_sem=sems[0].at[j],
                    recv_sem=sems[1].at[j], device_id={"seq": me + ring}, device_id_type=MESH,
                ).wait_send()


def wrapped(body, *refs):
    tail = refs[-16:]
    pairs = [(tail[i], tail[i + 1]) for i in range(0, 16, 2)]
    body(*refs[:-16], *pairs)


def solution(mesh):
    n = mesh.shape["seq"]
    ring = 4
    layers = n // ring

    def on_device(queries, keys, values, log_forget, input_gate, ridge, gain, out_weight):
        tokens, features = queries.shape
        heads = log_forget.shape[0]
        dh = features // heads
        share = heads // ring
        rows, columns = out_weight.shape

        def scans(kind):
            return [
                pltpu.VMEM((heads, dh, dh), kind),
                pltpu.VMEM((ring, share, dh, dh), kind),
                pltpu.VMEM((share, dh, dh), kind),
                pltpu.VMEM((share, dh, dh), kind),
                pltpu.VMEM((ring, share, dh, dh), kind),
                pltpu.VMEM((heads, dh, dh), kind),
            ]

        def pair(*shape):
            return [pltpu.SemaphoreType.DMA(shape), pltpu.SemaphoreType.DMA(shape)]

        vmem = pl.BlockSpec(memory_space=pltpu.VMEM)
        hbm = pl.BlockSpec(memory_space=pltpu.HBM)
        smem = pl.BlockSpec(memory_space=pltpu.SMEM)
        return pl.pallas_call(
            functools.partial(wrapped, functools.partial(kernel, layers, ring, heads)),
            out_shape=jax.ShapeDtypeStruct((tokens, columns), BF16),
            in_specs=[hbm, hbm, hbm, hbm, hbm, smem, hbm, hbm],
            out_specs=vmem,
            scratch_shapes=[
                pltpu.VMEM((tokens, features), BF16),
                pltpu.VMEM((tokens, features), BF16),
                pltpu.VMEM((tokens, features), BF16),
                pltpu.VMEM((heads, tokens), F32),
                pltpu.VMEM((heads, tokens), F32),
                pltpu.VMEM((1, features), F32),
                pltpu.SemaphoreType.DMA((7,)),
                pltpu.VMEM((ring, heads, dh), F32),
                *scans(BF16),
                *scans(BF16),
                pltpu.VMEM((n * rows, columns), BF16),
                pltpu.VMEM((tokens, features), BF16),
                *pair(ring),
                *pair(2, ring),
                *pair(2, share),
                *pair(2, ring),
                *pair(layers),
                *pair(layers),
                *pair(layers * 2),
                *pair(layers * ring),
            ],
            compiler_params=pltpu.CompilerParams(
                collective_id=0, has_side_effects=True, vmem_limit_bytes=56 * 1024 * 1024),
        )(queries, keys, values, log_forget, input_gate, ridge, gain.reshape(1, features), out_weight)

    placed = (
        P(("parts", "seq"), None),
        P(("parts", "seq"), None),
        P(("parts", "seq"), None),
        P(None, ("parts", "seq")),
        P(None, ("parts", "seq")),
        P(),
        P(),
        P("seq", None),
    )
    return jax.shard_map(
        on_device, mesh=mesh, in_specs=placed, out_specs=P(("parts", "seq"), None), check_vma=False
    )
```
